32 devices in a mesh: sec: 4 (over y, x), own: 8 (over z, core).
Axes of the slice: x: 2, y: 2, z: 4, core: 2. Of those that a mesh axis runs over, the one named last changes fastest.
Arguments:
- right_sides: float32 [2, 128, 8192], P(None, None, ('sec', 'own')), may hold values from -6 to 6
- inv_diag: float32 [8192, 256], P(('sec', 'own')), may hold values from -1 to 2, as said below
- factor_tiles: bfloat16 [8192, 2048], P(('sec', 'own')), may hold values from -0.0625 to 0.0625
- structure: int32 [32, 8], P(('sec', 'own')), may hold values 0 or 1
- ancestor: int32 [4, 8], P('sec'), may hold values from 0 to 7, each once within a row
- carried: float32 [128, 8192], P(None, ('sec', 'own')), may hold values from -4 to 4
Outputs:
- solution: float32 [2, 128, 8192], P(None, None, ('sec', 'own'))
- carry_out: float32 [128, 8192], P(None, ('sec', 'own'))
The draws below stay inside these ranges and needn't reach their ends.
Inputs may be any that keep to these rules, and one draw needn't show every extreme that they name: `inv_diag`: each diagonal block is the identity plus a dense part of moderate size. `ancestor`: each row is a permutation of 0 to 7.
All inputs are finite; a program needn't handle non-finite values. No bound on the sum of `structure` on one device may be relied on, other than what follows from the above.
Results may differ from the reference program's by a relative error of at most 0.0003.
Values sent between devices are 32-bit elements; how exact they have to be, the bound alone decides.
A program may use at most 64 MiB of HBM per device.

```python
import math
import jax
import jax.numpy as jnp
from jax import lax

B = 256
CHAIN = 128
TICKS = 2
SECTIONS = 4
OWNERS = 8
ANC = 8
ROWS = 8192


def draw_inv_diag(key, part):
    noise = jnp.clip(jax.random.normal(key, (ROWS, B), jnp.float32), -4.0, 4.0)
    factor = 0.5
    identity = jnp.tile(jnp.eye(B, dtype=jnp.float32), (ROWS // B, 1))
    return identity + factor * noise / math.sqrt(B)


def plant(array, own_key, least, largest):
    longest = array.shape.index(max(array.shape))
    spots = []
    for shift in (0, 1):
        where = [jax.random.randint(jax.random.fold_in(own_key, axis), (), 0, length) for axis, length in enumerate(array.shape)]
        where[longest] = (where[longest] + shift) % array.shape[longest]
        spots.append(tuple(where))
    return array.at[spots[0]].set(least).at[spots[1]].set(largest)


def block_scale(stream_key, shape, split, least, largest):
    def one(dim, blocks):
        draws = jax.random.uniform(jax.random.fold_in(jax.random.fold_in(stream_key, 6), dim), (blocks,), jnp.float32, least / len(split), largest / len(split))
        return jnp.repeat(jnp.exp(draws), shape[dim] // blocks).reshape((-1,) + (1,) * (len(shape) - dim - 1))

    factor_of = one(*split[0])
    for cut in split[1:]:
        factor_of = factor_of * one(*cut)
    return factor_of


def bell_draw(key, dims, width, reach, cuts=(), held_as=jnp.bfloat16):
    entries = jax.random.normal(key, dims, jnp.float32) * width
    if len(cuts) > 0:
        entries = block_scale(key, dims, cuts, -0.22, 0.18) * entries
    return jnp.clip(entries, min=-reach, max=reach).astype(held_as)


def setup_inputs(seed: int = 0) -> dict:
    keys = jax.random.split(jax.random.key(seed), 7)
    right_sides = bell_draw(keys[0], (TICKS, CHAIN, ROWS), 1.0, 6.0, ((2, 32),), jnp.float32)
    inv_diag = draw_inv_diag(jax.random.fold_in(keys[6], 71), 0)
    factor_tiles = bell_draw(keys[2], (ROWS, ANC * B), (4 * B * OWNERS) ** -0.5, 0.0625, ((0, 32),))
    structure = plant((jax.random.randint(keys[3], (SECTIONS * OWNERS, ANC), 0, 4) < 3).astype(jnp.int32), jax.random.fold_in(keys[3], 1), 0, 1)
    ancestor = jax.vmap(lambda own: jax.random.permutation(own, ANC))(jax.random.split(keys[4], SECTIONS)).reshape((SECTIONS, ANC)).astype(jnp.int32)
    carried = bell_draw(keys[5], (CHAIN, ROWS), 0.5, 4.0, ((1, 32),), jnp.float32)
    return dict(right_sides=right_sides, inv_diag=inv_diag, factor_tiles=factor_tiles, structure=structure, ancestor=ancestor, carried=carried)


def reference(right_sides, inv_diag, factor_tiles, structure, ancestor, carried):
    blocks = SECTIONS * OWNERS
    highest = lax.Precision.HIGHEST
    inverse = inv_diag.reshape(blocks, B, B)
    factor = factor_tiles.astype(jnp.float32).reshape(blocks, B, ANC * B)
    slot_target = jnp.repeat(ancestor, OWNERS, axis=0)
    selector = structure.astype(jnp.float32)[:, :, None] * (slot_target[:, :, None] == jnp.arange(ANC, dtype=jnp.int32)[None, None, :]).astype(jnp.float32)
    incoming = carried.reshape(CHAIN, blocks, B)
    solved_all = []
    for tick_index in range(TICKS):
        residual = right_sides[tick_index].reshape(CHAIN, blocks, B) - incoming
        solved = jnp.einsum('cki,kij->ckj', residual, inverse, precision=highest)
        solved_all.append(solved.reshape(CHAIN, ROWS))
        partial_value = jnp.einsum('cki,kin->ckn', solved, factor, precision=highest).reshape(CHAIN, blocks, ANC, B)
        routed = jnp.einsum('ckab,kaj->ckjb', partial_value, selector, precision=highest)
        per_section = routed.reshape(CHAIN, SECTIONS, OWNERS, ANC, B).sum(axis=2)
        shifted = jnp.concatenate([jnp.zeros((CHAIN, 1, ANC, B), jnp.float32), per_section[:, :-1]], axis=1)
        incoming = shifted.reshape(CHAIN, blocks, B)
    return jnp.stack(solved_all), incoming.reshape(CHAIN, ROWS)
```

```python
import functools

import jax
import jax.numpy as jnp
from jax import lax
from jax.experimental import pallas as pl
from jax.experimental.pallas import tpu as pltpu
from jax.sharding import PartitionSpec as P

MESH = pl.DeviceIdType.MESH
GROUPS = 2


def halves(x):
    high = x.astype(jnp.bfloat16)
    low = (x - high.astype(jnp.float32)).astype(jnp.bfloat16)
    return high, low


def kernel(
    sections, chips, groups, rs_hbm, d_hbm, f_hbm, st_ref, an_ref, ca_hbm, sol_ref, co_ref,
    rs, d, f, ca, part, other, up_in, down_in, hop_in,
    in_sem, xs, xr, us, ur, ds, dr, hs, hr,
):
    ticks, chain, block = rs.shape
    rows = chain // groups
    slots = an_ref.shape[1]
    sec, own = lax.axis_index("sec"), lax.axis_index("own")
    z, c = own // 2, own % 2
    loads = [
        pltpu.make_async_copy(src, dst, in_sem.at[i])
        for i, (src, dst) in enumerate(((rs_hbm, rs), (ca_hbm, ca), (d_hbm, d)))
    ]
    loads += [
        pltpu.make_async_copy(f_hbm.at[:, pl.ds(a * block, block)], f.at[a], in_sem.at[3 + a])
        for a in range(slots)
    ]
    for load in loads:
        load.start()

    partner = own + 1 - 2 * c
    greets = [
        (None, {"own": partner}),
        (z > 0, {"own": own - 2}),
        (z < chips - 1, {"own": own + 2}),
        (sec > 0, {"sec": sec - 1}),
        (sec < sections - 1, {"sec": sec + 1}),
    ]
    barrier = pltpu.get_barrier_semaphore()
    for there, device in greets:
        def greet(device=device):
            pl.semaphore_signal(barrier, inc=1, device_id=device, device_id_type=MESH)
        if there is None:
            greet()
        else:
            pl.when(there)(greet)
    peers = 1
    for there, _ in greets[1:]:
        peers = peers + there.astype(jnp.int32)
    pl.semaphore_wait(barrier, peers)

    active = sec < sections - 1

    def remote(src, dst, send, recv, device):
        return pltpu.make_async_remote_copy(
            src_ref=src, dst_ref=dst, send_sem=send, recv_sem=recv,
            device_id=device, device_id_type=MESH,
        )

    def swap(n, dst):
        return remote(part.at[n, 1 - c, dst], other.at[n, dst], xs.at[n, dst], xr.at[n, dst], {"own": partner})

    def up(n, dst):
        return remote(part.at[n, c, dst], up_in.at[n, dst], us.at[n, dst], ur.at[n, dst], {"own": own + 2})

    def down(n, dst):
        return remote(part.at[n, c, dst], down_in.at[n, dst], ds.at[n, dst], dr.at[n, dst], {"own": own - 2})

    def hop(n):
        return remote(part.at[n, c, z], hop_in.at[n], hs.at[n], hr.at[n], {"sec": sec + 1})

    order = []
    for i in range(chips):
        order.append(chips - 1 - i // 2 if i % 2 == 0 else i // 2)

    def slot_of(j):
        found, present = jnp.int32(0), jnp.int32(0)
        for a in range(slots):
            here = (an_ref[0, a] == j).astype(jnp.int32)
            found = found + here * a
            present = present + here * st_ref[0, a]
        return jnp.minimum(found, slots - 1), present.astype(jnp.float32)

    where = {}
    for side in (0, 1):
        for dst in order:
            where[side, dst] = slot_of(2 * dst + (1 - c if side == 0 else c))

    for load in loads[:3]:
        load.wait()
    d_high, d_low = halves(d[...])

    def start(n):
        t, g = divmod(n, groups)
        span = pl.ds(g * rows, rows)
        if t == 0:
            x = rs[t, span, :] - ca[span, :]
        else:
            @pl.when(sec > 0)
            def _():
                hop(n - groups).wait_recv()
                rs[t, span, :] = rs[t, span, :] - hop_in[n - groups]
            x = rs[t, span, :]
        x_high, x_low = halves(x)
        both = jnp.dot(
            jnp.concatenate([x_high, x_low], axis=0), d_high, preferred_element_type=jnp.float32
        )
        solved = both[:rows] + both[rows:] + jnp.dot(x_high, d_low, preferred_element_type=jnp.float32)
        sol_ref[t, span, :] = solved
        if n == 0:
            for load in loads[3:]:
                load.wait()

        @pl.when(active)
        def _():
            stacked = jnp.concatenate(halves(solved), axis=0)
            for side in (0, 1):
                for dst in order:
                    at, there = where[side, dst]
                    out = jnp.dot(
                        stacked, f[at], preferred_element_type=jnp.float32
                    )
                    part[n, 1 - c if side == 0 else c, dst] = (out[:rows] + out[rows:]) * there
                    if side == 0:
                        swap(n, dst).start()

    def forward(n, tau):
        @pl.when(active & (tau >= z))
        def _():
            dst = chips - 1 - tau + z
            swap(n, dst).wait_recv()

            @pl.when(z > 0)
            def _():
                up(n, dst).wait_recv()
                part[n, c, dst] = part[n, c, dst] + other[n, dst] + up_in[n, dst]

            @pl.when(z == 0)
            def _():
                part[n, c, dst] = part[n, c, dst] + other[n, dst]

            up(n, dst).start()

        @pl.when(active & (tau >= chips - 1 - z))
        def _():
            dst = tau - (chips - 1 - z)
            swap(n, dst).wait_recv()

            @pl.when(z < chips - 1)
            def _():
                down(n, dst).wait_recv()
                part[n, c, dst] = part[n, c, dst] + other[n, dst] + down_in[n, dst]

            @pl.when(z == chips - 1)
            def _():
                part[n, c, dst] = part[n, c, dst] + other[n, dst]

            down(n, dst).start()

    def finish(n):
        @pl.when(active)
        def _():
            swap(n, z).wait_recv()
            part[n, c, z] = part[n, c, z] + other[n, z]

            @pl.when(z > 0)
            def _():
                up(n, z).wait_recv()
                part[n, c, z] = part[n, c, z] + up_in[n, z]

            @pl.when(z < chips - 1)
            def _():
                down(n, z).wait_recv()
                part[n, c, z] = part[n, c, z] + down_in[n, z]

            hop(n).start()

    steps = ticks * groups
    for n in range(steps):
        if n >= 1 and groups == 1:
            finish(n - 1)
        start(n)
        forward(n, 0)
        if n >= 1 and groups > 1:
            finish(n - 1)
        for tau in range(1, chips - 1):
            forward(n, tau)
    finish(steps - 1)

    @pl.when(sec == 0)
    def _():
        co_ref[...] = jnp.zeros_like(co_ref)

    for g in range(groups):
        @pl.when(sec > 0)
        def _(g=g):
            n = (ticks - 1) * groups + g
            hop(n).wait_recv()
            co_ref[pl.ds(g * rows, rows), :] = hop_in[n]

    @pl.when(active)
    def _():
        for n in range(steps):
            hop(n).wait_send()
            for dst in range(chips):
                swap(n, dst).wait_send()
                pl.when(z < dst)(lambda n=n, dst=dst: up(n, dst).wait_send())
                pl.when(z > dst)(lambda n=n, dst=dst: down(n, dst).wait_send())


def solution(mesh):
    sections, owners = mesh.shape["sec"], mesh.shape["own"]
    chips = owners // 2

    def shards(right_sides, inv_diag, factor_tiles, structure, ancestor, carried):
        ticks, chain, block = right_sides.shape
        slots = structure.shape[1]
        steps, rows = ticks * GROUPS, chain // GROUPS
        flag = pltpu.SemaphoreType.DMA
        f32 = jnp.float32
        hbm = pl.BlockSpec(memory_space=pl.ANY)
        smem = pl.BlockSpec(memory_space=pltpu.SMEM)
        vmem = pl.BlockSpec(memory_space=pltpu.VMEM)
        return pl.pallas_call(
            functools.partial(kernel, sections, chips, GROUPS),
            out_shape=(
                jax.ShapeDtypeStruct(right_sides.shape, f32),
                jax.ShapeDtypeStruct(carried.shape, f32),
            ),
            in_specs=[hbm, hbm, hbm, smem, smem, hbm],
            out_specs=(vmem, vmem),
            scratch_shapes=[
                pltpu.VMEM(right_sides.shape, f32),
                pltpu.VMEM(inv_diag.shape, f32),
                pltpu.VMEM((slots, block, block), factor_tiles.dtype),
                pltpu.VMEM(carried.shape, f32),
                pltpu.VMEM((steps, 2, chips, rows, block), f32),
                pltpu.VMEM((steps, chips, rows, block), f32),
                pltpu.VMEM((steps, chips, rows, block), f32),
                pltpu.VMEM((steps, chips, rows, block), f32),
                pltpu.VMEM((steps, rows, block), f32),
                flag((3 + slots,)),
                *[flag((steps, chips))] * 6,
                *[flag((steps,))] * 2,
            ],
            compiler_params=pltpu.CompilerParams(
                collective_id=0, has_side_effects=True, vmem_limit_bytes=40 * 1024 * 1024
            ),
        )(right_sides, inv_diag, factor_tiles, structure, ancestor, carried)

    in_specs = (
        P(None, None, ("sec", "own")),
        P(("sec", "own"), None),
        P(("sec", "own"), None),
        P(("sec", "own"), None),
        P("sec", None),
        P(None, ("sec", "own")),
    )
    out_specs = (P(None, None, ("sec", "own")), P(None, ("sec", "own")))
    return jax.shard_map(shards, mesh=mesh, in_specs=in_specs, out_specs=out_specs, check_vma=False)
```

```python
import functools

import jax
import jax.numpy as jnp
from jax import lax
from jax.experimental import pallas as pl
from jax.experimental.pallas import tpu as pltpu
from jax.sharding import PartitionSpec as P

MESH = pl.DeviceIdType.MESH
GROUPS = 2
LAG = 0.1


def halves(x):
    high = x.astype(jnp.bfloat16)
    low = (x - high.astype(jnp.float32)).astype(jnp.bfloat16)
    return high, low


def kernel(
    sections, chips, groups, rs_hbm, d_hbm, f_hbm, st_ref, an_ref, ca_hbm, sol_ref, co_ref,
    rs, d, f, ca, part, other, up_in, down_in, hop_in,
    in_sem, xs, xr, us, ur, ds, dr, hs, hr,
):
    ticks, chain, block = rs.shape
    rows = chain // groups
    slots = an_ref.shape[1]
    sec, own = lax.axis_index("sec"), lax.axis_index("own")
    z, c = own // 2, own % 2
    loads = [
        pltpu.make_async_copy(src, dst, in_sem.at[i])
        for i, (src, dst) in enumerate(((rs_hbm, rs), (ca_hbm, ca), (d_hbm, d)))
    ]
    loads += [
        pltpu.make_async_copy(f_hbm.at[:, pl.ds(a * block, block)], f.at[a], in_sem.at[3 + a])
        for a in range(slots)
    ]
    for load in loads:
        load.start()

    partner = own + 1 - 2 * c
    greets = [
        (None, {"own": partner}),
        (z > 0, {"own": own - 2}),
        (z < chips - 1, {"own": own + 2}),
        (sec > 0, {"sec": sec - 1}),
        (sec < sections - 1, {"sec": sec + 1}),
    ]
    barrier = pltpu.get_barrier_semaphore()
    for there, device in greets:
        def greet(device=device):
            pl.semaphore_signal(barrier, inc=1, device_id=device, device_id_type=MESH)
        if there is None:
            greet()
        else:
            pl.when(there)(greet)
    peers = 1
    for there, _ in greets[1:]:
        peers = peers + there.astype(jnp.int32)
    pl.semaphore_wait(barrier, peers)

    active = sec < sections - 1

    def remote(src, dst, send, recv, device):
        return pltpu.make_async_remote_copy(
            src_ref=src, dst_ref=dst, send_sem=send, recv_sem=recv,
            device_id=device, device_id_type=MESH,
        )

    def swap(n, dst):
        return remote(part.at[n, 1 - c, dst], other.at[n, dst], xs.at[n, dst], xr.at[n, dst], {"own": partner})

    def up(n, dst):
        return remote(part.at[n, c, dst], up_in.at[n, dst], us.at[n, dst], ur.at[n, dst], {"own": own + 2})

    def down(n, dst):
        return remote(part.at[n, c, dst], down_in.at[n, dst], ds.at[n, dst], dr.at[n, dst], {"own": own - 2})

    def hop(n):
        return remote(part.at[n, c, z], hop_in.at[n], hs.at[n], hr.at[n], {"sec": sec + 1})

    order = []
    for i in range(chips):
        order.append(chips - 1 - i // 2 if i % 2 == 0 else i // 2)

    def slot_of(j):
        found, present = jnp.int32(0), jnp.int32(0)
        for a in range(slots):
            here = (an_ref[0, a] == j).astype(jnp.int32)
            found = found + here * a
            present = present + here * st_ref[0, a]
        return jnp.minimum(found, slots - 1), present.astype(jnp.float32)

    where = {}
    for side in (0, 1):
        for dst in order:
            where[side, dst] = slot_of(2 * dst + (1 - c if side == 0 else c))

    for load in loads[:3]:
        load.wait()
    d_high, d_low = halves(d[...])

    def start(n):
        t, g = divmod(n, groups)
        span = pl.ds(g * rows, rows)
        if t == 0:
            x = rs[t, span, :] - ca[span, :]
        else:
            @pl.when(sec > 0)
            def _():
                hop(n - groups).wait_recv()
                rs[t, span, :] = rs[t, span, :] - hop_in[n - groups]
            x = rs[t, span, :]
        x_high, x_low = halves(x)
        both = jnp.dot(
            jnp.concatenate([x_high, x_low], axis=0), d_high, preferred_element_type=jnp.float32
        )
        solved = both[:rows] + both[rows:] + jnp.dot(x_high, d_low, preferred_element_type=jnp.float32)
        sol_ref[t, span, :] = solved
        if n == 0:
            for load in loads[3:]:
                load.wait()

        @pl.when(active)
        def _():
            stacked = jnp.concatenate(halves(solved), axis=0)
            for side in (0, 1):
                for dst in order:
                    at, there = where[side, dst]
                    out = jnp.dot(
                        stacked, f[at], preferred_element_type=jnp.float32
                    )
                    part[n, 1 - c if side == 0 else c, dst] = (out[:rows] + out[rows:]) * there
                    if side == 0:
                        swap(n, dst).start()

    def forward(n, tau):
        @pl.when(active & (tau >= z))
        def _():
            dst = chips - 1 - tau + z
            swap(n, dst).wait_recv()

            @pl.when(z > 0)
            def _():
                up(n, dst).wait_recv()
                part[n, c, dst] = part[n, c, dst] + other[n, dst] + up_in[n, dst]

            @pl.when(z == 0)
            def _():
                part[n, c, dst] = part[n, c, dst] + other[n, dst]

            up(n, dst).start()

        @pl.when(active & (tau >= chips - 1 - z))
        def _():
            dst = tau - (chips - 1 - z)
            swap(n, dst).wait_recv()

            @pl.when(z < chips - 1)
            def _():
                down(n, dst).wait_recv()
                part[n, c, dst] = part[n, c, dst] + other[n, dst] + down_in[n, dst]

            @pl.when(z == chips - 1)
            def _():
                part[n, c, dst] = part[n, c, dst] + other[n, dst]

            down(n, dst).start()

    def finish(n):
        @pl.when(active)
        def _():
            swap(n, z).wait_recv()
            part[n, c, z] = part[n, c, z] + other[n, z]

            @pl.when(z > 0)
            def _():
                up(n, z).wait_recv()
                part[n, c, z] = part[n, c, z] + up_in[n, z]

            @pl.when(z < chips - 1)
            def _():
                down(n, z).wait_recv()
                part[n, c, z] = part[n, c, z] + down_in[n, z]

            hop(n).start()

    steps = ticks * groups
    waves = chips - 1
    period = waves * groups + 1 + min(groups - 1, 2) + 0.5
    plan = []
    for n in range(steps):
        t, g = divmod(n, groups)
        first = t * period + g
        plan.append((first, functools.partial(start, n)))
        for tau in range(waves):
            plan.append((first + LAG + tau * groups, functools.partial(forward, n, tau)))
        plan.append((first + LAG + waves * groups, functools.partial(finish, n)))
    for _, event in sorted(plan, key=lambda entry: entry[0]):
        event()

    @pl.when(sec == 0)
    def _():
        co_ref[...] = jnp.zeros_like(co_ref)

    for g in range(groups):
        @pl.when(sec > 0)
        def _(g=g):
            n = (ticks - 1) * groups + g
            hop(n).wait_recv()
            co_ref[pl.ds(g * rows, rows), :] = hop_in[n]

    @pl.when(active)
    def _():
        for n in range(steps):
            hop(n).wait_send()
            for dst in range(chips):
                swap(n, dst).wait_send()
                pl.when(z < dst)(lambda n=n, dst=dst: up(n, dst).wait_send())
                pl.when(z > dst)(lambda n=n, dst=dst: down(n, dst).wait_send())


def solution(mesh):
    sections, owners = mesh.shape["sec"], mesh.shape["own"]
    chips = owners // 2

    def shards(right_sides, inv_diag, factor_tiles, structure, ancestor, carried):
        ticks, chain, block = right_sides.shape
        slots = structure.shape[1]
        steps, rows = ticks * GROUPS, chain // GROUPS
        flag = pltpu.SemaphoreType.DMA
        f32 = jnp.float32
        hbm = pl.BlockSpec(memory_space=pl.ANY)
        smem = pl.BlockSpec(memory_space=pltpu.SMEM)
        vmem = pl.BlockSpec(memory_space=pltpu.VMEM)
        return pl.pallas_call(
            functools.partial(kernel, sections, chips, GROUPS),
            out_shape=(
                jax.ShapeDtypeStruct(right_sides.shape, f32),
                jax.ShapeDtypeStruct(carried.shape, f32),
            ),
            in_specs=[hbm, hbm, hbm, smem, smem, hbm],
            out_specs=(vmem, vmem),
            scratch_shapes=[
                pltpu.VMEM(right_sides.shape, f32),
                pltpu.VMEM(inv_diag.shape, f32),
                pltpu.VMEM((slots, block, block), factor_tiles.dtype),
                pltpu.VMEM(carried.shape, f32),
                pltpu.VMEM((steps, 2, chips, rows, block), f32),
                pltpu.VMEM((steps, chips, rows, block), f32),
                pltpu.VMEM((steps, chips, rows, block), f32),
                pltpu.VMEM((steps, chips, rows, block), f32),
                pltpu.VMEM((steps, rows, block), f32),
                flag((3 + slots,)),
                *[flag((steps, chips))] * 6,
                *[flag((steps,))] * 2,
            ],
            compiler_params=pltpu.CompilerParams(
                collective_id=0, has_side_effects=True, vmem_limit_bytes=62 * 1024 * 1024
            ),
        )(right_sides, inv_diag, factor_tiles, structure, ancestor, carried)

    in_specs = (
        P(None, None, ("sec", "own")),
        P(("sec", "own"), None),
        P(("sec", "own"), None),
        P(("sec", "own"), None),
        P("sec", None),
        P(None, ("sec", "own")),
    )
    out_specs = (P(None, None, ("sec", "own")), P(None, ("sec", "own")))
    return jax.shard_map(shards, mesh=mesh, in_specs=in_specs, out_specs=out_specs, check_vma=False)
```
